32 devices in a mesh: gx: 8 (over y, x, core), gy: 4 (over z).
Axes of the slice: x: 2, y: 2, z: 4, core: 2. Of those that a mesh axis runs over, the one named last changes fastest.
Arguments:
- records: bfloat16 [32, 32, 64, 128], P(('gx', 'gy')), may hold values from -6 to 6
- slot_voxels: int32 [32, 32, 256], P(('gx', 'gy')), may hold values from 0 to 8192, as said below
- brick_mask: int32 [16, 8, 4], P('gx', 'gy'), may hold values 0 or 1
- lift_weight: bfloat16 [32, 64], replicated, may hold values from -1 to 1
- leaf_convs: bfloat16 [2, 3, 3, 3, 64, 64], replicated, may hold values from -0.21875 to 0.21875
- down_leaf: bfloat16 [2, 2, 2, 64, 128], replicated, may hold values from -0.375 to 0.375
- down_coarse: bfloat16 [2, 2, 2, 2, 128, 128], replicated, may hold values from -0.25 to 0.25
- coarse_convs: bfloat16 [3, 3, 3, 3, 128, 128], replicated, may hold values from -0.15625 to 0.15625
Outputs:
- leaf_features: bfloat16 [128, 64, 16, 128], P('gx', 'gy')
- top_features: bfloat16 [16, 8, 4, 128], P('gx', 'gy')
The draws below stay inside these ranges and needn't reach their ends.
Inputs may be any that keep to these rules, and one draw needn't show every extreme that they name: `slot_voxels`: entry [s, d, j] is owner d's local voxel index of slot j of the records that device s sends to owner d, or 8192 where that slot is empty; filled slots come first in each bucket; in every draw some owner receives 256 filled slots from every device, and every bucket has an empty slot unless its owner is such a full one.
All inputs are finite; a program needn't handle non-finite values. No bound on the sum of `brick_mask` on one device may be relied on, other than what follows from the above.
Results may differ from the reference program's by a relative error of at most 0.023.
Values may be sent and summed in bfloat16 or wider, within the bound.
A program may use at most 64 MiB of HBM per device.

```python
import jax
import jax.numpy as jnp
from jax import lax

FEAT = 32
CH_LEAF = 64
CH_COARSE = 128
BRICK = 8
BRICK_X = 2
BRICK_Y = 2
BRICK_Z = 4
CAP = 256
VOX_X = 16
VOX_Y = 16
VOX_Z = 32
VOXELS = 8192
GRID_X = 128
GRID_Y = 64
N_GX = 8
N_GY = 4
DEVICES = 32


def draw_slot_voxels(key, part):
    key_hot, key_forced, key_base, key_voxel = jax.random.split(key, 4)
    owner_hot = jax.random.randint(key_hot, (DEVICES,), 0, 4) == 0
    forced = jax.random.randint(key_forced, (), 0, DEVICES)
    owner_hot = owner_hot | (jnp.arange(DEVICES) == forced)
    base_count = jax.random.randint(key_base, (DEVICES, DEVICES), CAP // 8, CAP // 2 + 1)
    filled = jnp.where(owner_hot[None, :], CAP, base_count)
    voxel_draw = jax.random.randint(key_voxel, (DEVICES, DEVICES, CAP), 0, VOXELS)
    slot_index = jnp.arange(CAP)[None, None, :]
    return jnp.where(slot_index < filled[:, :, None], voxel_draw, VOXELS).astype(jnp.int32)


def set_ends(array, stream_key, least, largest):
    longest = array.shape.index(max(array.shape))
    spots = []
    for shift in (0, 1):
        where = [jax.random.randint(jax.random.fold_in(stream_key, axis), (), 0, length) for axis, length in enumerate(array.shape)]
        where[longest] = (where[longest] + shift) % array.shape[longest]
        spots.append(tuple(where))
    return array.at[spots[0]].set(least).at[spots[1]].set(largest)


def shard_levels(rng, dims, cuts, low, top_value):
    loudness, own = 1.0, jax.random.fold_in(rng, 6)
    for dim, parts in cuts:
        draws = jnp.exp(jax.random.uniform(jax.random.fold_in(own, dim), (parts,), jnp.float32, low / len(cuts), top_value / len(cuts)))
        loudness = loudness * jnp.repeat(draws, dims[dim] // parts).reshape([-1 if axis == dim else 1 for axis in range(len(dims))])
    return loudness


def gaussian(own_key, extent, deviation, most, cuts=(), kind=jnp.bfloat16):
    drawn = deviation * jax.random.normal(own_key, extent, jnp.float32)
    if cuts:
        drawn = drawn * shard_levels(own_key, extent, cuts, -0.22, 0.18)
    return jnp.clip(drawn, -most, most).astype(kind)


def setup_inputs(seed: int = 0) -> dict:
    seeds = jax.random.split(jax.random.key(seed), 9)
    return {
        "records": gaussian(seeds[0], (DEVICES, DEVICES, CAP // 4, 4 * FEAT), 1.0, 6.0, ((0, 32),)),
        "slot_voxels": draw_slot_voxels(jax.random.fold_in(seeds[8], 71), 0),
        "brick_mask": set_ends((jax.random.randint(seeds[2], (BRICK_X * N_GX, BRICK_Y * N_GY, BRICK_Z), 0, 4) < 3).astype(jnp.int32), jax.random.fold_in(seeds[2], 1), 0, 1),
        "lift_weight": gaussian(seeds[3], (FEAT, CH_LEAF), FEAT ** -0.5, 1.0),
        "leaf_convs": gaussian(seeds[4], (2, 3, 3, 3, CH_LEAF, CH_LEAF), (27 * CH_LEAF // 2) ** -0.5, 0.21875),
        "down_leaf": gaussian(seeds[5], (2, 2, 2, CH_LEAF, CH_COARSE), (4 * CH_LEAF) ** -0.5, 0.375),
        "down_coarse": gaussian(seeds[6], (2, 2, 2, 2, CH_COARSE, CH_COARSE), (4 * CH_COARSE) ** -0.5, 0.25),
        "coarse_convs": gaussian(seeds[7], (3, 3, 3, 3, CH_COARSE, CH_COARSE), (27 * CH_COARSE // 2) ** -0.5, 0.15625),
    }


def conv_cube(values, kernel):
    padded = jnp.pad(values, ((1, 1), (1, 1), (1, 1), (0, 0)))
    size_a, size_b, size_c, channels = values.shape
    summed = jnp.zeros((size_a * size_b * size_c, kernel.shape[-1]), jnp.float32)
    for step_x in range(3):
        for step_y in range(3):
            for step_z in range(3):
                window = padded[step_x:step_x + size_a, step_y:step_y + size_b, step_z:step_z + size_c]
                summed = summed + jnp.dot(window.reshape(-1, channels), kernel[step_x, step_y, step_z], preferred_element_type=jnp.float32)
    return summed.reshape(size_a, size_b, size_c, kernel.shape[-1])


def shrink_cube(values, kernel):
    size_a, size_b, size_c, channels = values.shape
    blocks = values.astype(jnp.float32).reshape(size_a // 2, 2, size_b // 2, 2, size_c // 2, 2, channels)
    return jnp.einsum("xaybzci,abcio->xyzo", blocks, kernel.astype(jnp.float32), precision=lax.Precision.HIGHEST)


def expand_mask(brick_mask, factor):
    widened_mask = jnp.repeat(jnp.repeat(jnp.repeat(brick_mask, factor, 0), factor, 1), factor, 2)
    return widened_mask.astype(jnp.float32)[..., None]


def reference(records, slot_voxels, brick_mask, lift_weight, leaf_convs, down_leaf, down_coarse, coarse_convs):
    owners = jnp.arange(DEVICES, dtype=jnp.int32)[None, :, None]
    owner_x = owners // N_GY
    owner_y = owners % N_GY
    coord_x = owner_x * VOX_X + slot_voxels // (VOX_Y * VOX_Z)
    coord_y = owner_y * VOX_Y + (slot_voxels // VOX_Z) % VOX_Y
    coord_z = slot_voxels % VOX_Z
    cell_count = GRID_X * GRID_Y * VOX_Z
    target = (coord_x * GRID_Y + coord_y) * VOX_Z + coord_z
    target = jnp.where(slot_voxels < VOXELS, target, cell_count).astype(jnp.int32).reshape(-1)
    flat_records = records.reshape(-1, FEAT).astype(jnp.float32)
    summed = jax.ops.segment_sum(flat_records, target, num_segments=cell_count + 1)[:cell_count]
    lifted = jnp.dot(summed, lift_weight.astype(jnp.float32), precision=lax.Precision.HIGHEST)
    hidden = lifted.reshape(GRID_X, GRID_Y, VOX_Z, CH_LEAF).astype(jnp.bfloat16)
    leaf_occupied = expand_mask(brick_mask, BRICK)
    for layer_index in range(2):
        hidden = (jax.nn.relu(conv_cube(hidden, leaf_convs[layer_index])) * leaf_occupied).astype(jnp.bfloat16)
    leaf_features = hidden.reshape(GRID_X, GRID_Y, VOX_Z // 2, 2 * CH_LEAF)
    for level_index in range(3):
        factor = BRICK // 2 ** (level_index + 1)
        occupied = expand_mask(brick_mask, factor)
        kernel = down_leaf if level_index == 0 else down_coarse[level_index - 1]
        hidden = (jax.nn.relu(shrink_cube(hidden, kernel)) * occupied).astype(jnp.bfloat16)
        hidden = (jax.nn.relu(conv_cube(hidden, coarse_convs[level_index])) * occupied).astype(jnp.bfloat16)
    return leaf_features, hidden
```

```python
import functools

import jax
import jax.numpy as jnp
from jax import lax
from jax.experimental import pallas as pl
from jax.experimental.pallas import tpu as pltpu
from jax.sharding import PartitionSpec as P

BRICK = 8
F32 = jnp.float32
BF16 = jnp.bfloat16
SIDES = [(-1, 0), (1, 0), (0, -1), (0, 1), (-1, -1), (-1, 1), (1, -1), (1, 1)]


def dot(left, right):
    return jnp.dot(left, right, preferred_element_type=F32)


def leaf_taps(kernels):
    low, mid, high = kernels[:, :, :, 0], kernels[:, :, :, 1], kernels[:, :, :, 2]
    none = jnp.zeros_like(low)
    first = jnp.concatenate([mid, high, none, low], -2)
    second = jnp.concatenate([low, mid, high, none], -2)
    taps = jnp.concatenate([first, second], -1)
    return taps.reshape(taps.shape[0], 9, taps.shape[3], taps.shape[4])


def lift_blocks(lift_weight, copies):
    feature_count, channels = lift_weight.shape
    tiled = jnp.tile(lift_weight, (copies, copies))
    row = lax.broadcasted_iota(jnp.int32, tiled.shape, 0) // feature_count
    column = lax.broadcasted_iota(jnp.int32, tiled.shape, 1) // channels
    return jnp.where(row == column, tiled, 0)


def spread(mask, factor, factor_z, pad_z=0):
    wide = jnp.repeat(jnp.repeat(mask, factor, 0), factor, 1)
    wide = jnp.repeat(wide, factor_z, 2).astype(F32)
    wide = jnp.pad(wide, ((0, 0), (0, 0), (0, pad_z)))
    return jnp.broadcast_to(wide[..., None], wide.shape + (128,))


def side_parts(count, here, other):
    near, far = 1, count
    own = {-1: near, 1: far, 0: pl.ds(1, count)}
    there = {-1: count + 1, 1: 0, 0: pl.ds(1, count)}
    return (own[here], own[other]), (there[here], there[other])


class Halo:
    def __init__(self, size_x, size_y, send_sems, recv_sems):
        self.place_x, self.place_y = lax.axis_index("gx"), lax.axis_index("gy")
        self.size_x, self.size_y = size_x, size_y
        self.send_sems, self.recv_sems = send_sems, recv_sems

    def each(self, action):
        for index, (step_x, step_y) in enumerate(SIDES):
            to_x, to_y = self.place_x + step_x, self.place_y + step_y
            tests = []
            if step_x:
                tests.append(to_x >= 0 if step_x < 0 else to_x < self.size_x)
            if step_y:
                tests.append(to_y >= 0 if step_y < 0 else to_y < self.size_y)
            exists = tests[0] if len(tests) == 1 else jnp.logical_and(*tests)

            @pl.when(exists)
            def _():
                action(index, step_x, step_y, (to_x, to_y))

    def barrier(self):
        semaphore = pltpu.get_barrier_semaphore()

        def signal(index, step_x, step_y, target):
            pl.semaphore_signal(
                semaphore, inc=1, device_id=target, device_id_type=pl.DeviceIdType.MESH
            )

        def near(place, size):
            before = jnp.where(place > 0, 1, 0)
            return before + jnp.where(place < size - 1, 1, 0)

        self.each(signal)
        columns = near(self.place_x, self.size_x) + 1
        pl.semaphore_wait(semaphore, columns * (near(self.place_y, self.size_y) + 1) - 1)

    def copy(self, stage, buffer, index, step_x, step_y, target):
        source, landing = side_parts(buffer.shape[0] - 2, step_x, step_y)
        return pltpu.make_async_remote_copy(
            src_ref=buffer.at[source],
            dst_ref=buffer.at[landing],
            send_sem=self.send_sems.at[stage, index],
            recv_sem=self.recv_sems.at[stage, index],
            device_id=target,
            device_id_type=pl.DeviceIdType.MESH,
        )

    def start(self, stage, buffer):
        self.each(lambda *where: self.copy(stage, buffer, *where).start())

    def wait_arrived(self, stage, buffer):
        def arrived(index, step_x, step_y, target):
            opposite = SIDES.index((-step_x, -step_y))
            self.copy(stage, buffer, opposite, -step_x, -step_y, target).wait_recv()

        self.each(arrived)

    def wait_sent(self, stage, buffer):
        self.each(lambda *where: self.copy(stage, buffer, *where).wait_send())


def clear_border(buffer):
    last = buffer.shape[0] - 1
    edge = jnp.zeros(buffer.shape[1:], buffer.dtype)
    column = jnp.zeros((buffer.shape[0],) + buffer.shape[2:], buffer.dtype)
    buffer[0] = edge
    buffer[last] = edge
    buffer[:, 0] = column
    buffer[:, last] = column


def shift_rows(rows, period):
    count = rows.shape[0]
    z = lax.broadcasted_iota(jnp.int32, rows.shape, 0) % period
    before = jnp.where(z == 0, 0.0, pltpu.roll(rows, 1, 0))
    after = jnp.where(z == period - 1, 0.0, pltpu.roll(rows, count - 1, 0))
    return before, after


def store_leaf(buffer, at_x, at_y, rows, shape):
    before, after = shift_rows(rows, shape[2])
    lane = lax.broadcasted_iota(jnp.int32, rows.shape, 1)
    outer = jnp.where(lane < rows.shape[1] // 2, after, before)
    both = jnp.concatenate([rows, outer], -1).astype(BF16)
    buffer[at_x, at_y] = both.reshape(shape[:3] + (both.shape[-1],))


def stacked_z(values):
    shape = values.shape
    rows = values.reshape(-1, shape[-1])
    before, after = shift_rows(rows, shape[2])
    return jnp.concatenate([before, rows, after], -1).reshape(shape[:3] + (3 * shape[3],))


def pair_part(values, part_x, part_y):
    size_x, size_y = values.shape[:2]
    split = values.reshape((size_x // 2, 2, size_y // 2, 2) + values.shape[2:])
    return split[:, part_x, :, part_y]


def encoder(
    n_gx,
    n_gy,
    arrived,
    slots,
    lift,
    taps,
    down_leaf,
    down_coarse,
    coarse_convs,
    occ0,
    occ1,
    occ2,
    occ3,
    leaf_out,
    top_out,
    summed,
    leaf_a,
    leaf_b,
    coarse_a,
    coarse_b,
    coarse_c,
    stacked,
    level_one,
    level_two,
    send_sems,
    recv_sems,
):
    halo = Halo(n_gx, n_gy, send_sems, recv_sems)
    for buffer in (leaf_a, leaf_b, coarse_a, coarse_b, coarse_c):
        clear_border(buffer)
    halo.barrier()

    senders, slot_rows, width = arrived.shape
    cap = slots.shape[1]
    lanes = cap // slot_rows
    features = width // lanes
    span = summed.shape[1]
    rows_hi = summed.shape[0]
    group = 4
    order_from = lax.broadcasted_iota(jnp.int32, (cap, cap), 0)
    order_to = lax.broadcasted_iota(jnp.int32, (cap, cap), 1)
    order = jnp.where(
        order_from == (order_to % slot_rows) * lanes + order_to // slot_rows, 1.0, 0.0
    ).astype(BF16)
    pick_from = lax.broadcasted_iota(jnp.int32, (width, lanes * span), 0)
    pick_to = lax.broadcasted_iota(jnp.int32, (width, lanes * span), 1)
    pick = jnp.where(
        pick_from == (pick_to // span) * features + pick_to % features, 1.0, 0.0
    ).astype(BF16)
    column_group = (
        lax.broadcasted_iota(jnp.int32, (cap, span), 1) // features
    ).astype(F32)
    row_index = lax.broadcasted_iota(jnp.int32, (rows_hi, cap), 0).astype(F32)
    summed[...] = jnp.zeros_like(summed)

    def add_group(step, carry):
        base = pl.multiple_of(step * 8, 8)
        index = slots[pl.ds(base, 8), :]
        half = index // 2
        high = half % rows_hi
        low = (index // (2 * rows_hi)) * 2 + index % 2
        high_row = 64.0 * dot((high // 64).astype(F32).astype(BF16), order) + dot(
            (high % 64).astype(F32).astype(BF16), order
        )
        low_column = lax.dot_general(
            order,
            low.astype(F32).astype(BF16),
            (((0,), (1,)), ((), ())),
            preferred_element_type=F32,
        )
        for part in range(8 // group):
            hots, tables = [], []
            for inner in range(group):
                place = part * group + inner
                hot = jnp.where(row_index == high_row[place : place + 1], 1.0, 0.0)
                hots.append(hot.astype(BF16))
                wide = dot(arrived[base + place], pick)
                wide = jnp.concatenate(
                    [wide[:, lane * span : (lane + 1) * span] for lane in range(lanes)], 0
                )
                tables.append(
                    jnp.where(column_group == low_column[:, place : place + 1], wide, 0.0).astype(
                        BF16
                    )
                )
            summed[...] += dot(jnp.concatenate(hots, 1), jnp.concatenate(tables, 0))
        return carry

    lax.fori_loop(0, senders // 8, add_group, 0)

    size_x, size_y, size_z, leaf_width = leaf_out.shape
    quarter = rows_hi // (size_y * size_z)
    rest = summed[...]
    lifted = 0.0
    for piece in range(3):
        cut = rest.astype(BF16)
        rest = rest - cut.astype(F32)
        lifted = lifted + dot(cut, lift[...])
    inside_y = pl.ds(1, size_y)
    for block in range(size_x // quarter):
        store_leaf(
            leaf_a,
            pl.ds(1 + block * quarter, quarter),
            inside_y,
            lifted[:, block * leaf_width : (block + 1) * leaf_width],
            (quarter, size_y, size_z),
        )

    halo.start(0, leaf_a)

    def convolve(source, layer, x, count_x, y, count_y):
        total = None
        for step in range(9):
            window = source[pl.ds(x + step // 3, count_x), pl.ds(y + step % 3, count_y)]
            term = dot(window.reshape(-1, window.shape[-1]), taps[layer, step])
            total = term if total is None else total + term
        return jnp.maximum(total, 0.0)

    def leaf_layer(source, layer, emit):
        def block(x, count_x, y, count_y):
            swept = convolve(source, layer, x, count_x, y, count_y)
            occupied = jnp.concatenate(
                [
                    occ0[pl.ds((x + step) // BRICK, 1), y : y + count_y]
                    for step in range(count_x)
                ],
                0,
            )
            emit(x, count_x, y, count_y, swept * occupied.reshape(swept.shape))

        def inner(step, carry):
            block(1 + 2 * step, 2, 1, size_y - 2)
            return carry

        lax.fori_loop(0, (size_x - 2) // 2, inner, 0)
        halo.wait_arrived(layer, source)
        block(0, 1, 0, size_y)
        block(size_x - 1, 1, 0, size_y)
        block(1, size_x - 2, 0, 1)
        block(1, size_x - 2, size_y - 1, 1)

    def keep_first(x, count_x, y, count_y, rows):
        store_leaf(
            leaf_b,
            pl.ds(1 + x, count_x),
            pl.ds(1 + y, count_y),
            rows,
            (count_x, count_y, size_z),
        )

    def keep_second(x, count_x, y, count_y, rows):
        leaf_out[pl.ds(x, count_x), pl.ds(y, count_y)] = rows.astype(BF16).reshape(
            count_x, count_y, size_z, leaf_width
        )

    leaf_layer(leaf_a, 0, keep_first)
    halo.start(1, leaf_b)
    leaf_layer(leaf_b, 1, keep_second)

    def coarse_conv(level, kernel, occupied):
        count, depth = kernel.shape[0] - 2, kernel.shape[2]
        total = None
        for step in range(9):
            step_x, step_y = step // 3, step % 3
            window = kernel[step_x : step_x + count, step_y : step_y + count]
            window = window.reshape(count * count * depth, window.shape[-1]).astype(BF16)
            term = dot(window, coarse_convs[level, step])
            total = term if total is None else total + term
        return jnp.maximum(total, 0.0).reshape(occupied.shape) * occupied[...]

    def finish_down(stage, buffer, total, occupied):
        count = occupied.shape[0]
        cells = jnp.maximum(total, 0.0).reshape(occupied.shape) * occupied[...]
        buffer[1 : count + 1, 1 : count + 1] = cells
        halo.start(stage, buffer)
        halo.wait_arrived(stage, buffer)

    total = 0.0
    leaf = leaf_out[...]
    for part in range(4):
        piece = pair_part(leaf, part // 2, part % 2)
        total = total + dot(piece.reshape(-1, leaf_width), down_leaf[part])
    finish_down(2, coarse_a, total, occ1)
    stacked[...] = stacked_z(coarse_a[...]).astype(BF16)
    level_one[...] = coarse_conv(0, stacked, occ1)

    def shrink(level, source, depth):
        total = 0.0
        for part_z in range(2):
            half = source[:, :, pl.ds(part_z, depth, 2), :]
            for part in range(4):
                piece = pair_part(half, part // 2, part % 2)
                piece = piece.reshape(-1, piece.shape[-1]).astype(BF16)
                total = total + dot(piece, down_coarse[level, 2 * part + part_z])
        return total

    finish_down(3, coarse_b, shrink(0, level_one, occ2.shape[2]), occ2)
    deep = occ2.shape[2]
    level_two[:, :, deep : 2 * deep] = jnp.zeros_like(occ2)
    level_two[:, :, 0:deep] = coarse_conv(1, stacked_z(coarse_b[...]), occ2)
    finish_down(4, coarse_c, shrink(1, level_two, occ3.shape[2]), occ3)
    top_out[...] = coarse_conv(2, stacked_z(coarse_c[...]), occ3)

    for stage, buffer in enumerate((leaf_a, leaf_b, coarse_a, coarse_b, coarse_c)):
        halo.wait_sent(stage, buffer)


def per_device(
    n_gx,
    n_gy,
    records,
    slot_voxels,
    brick_mask,
    lift_weight,
    leaf_convs,
    down_leaf,
    down_coarse,
    coarse_convs,
):
    arrived = lax.all_to_all(records[0], ("gx", "gy"), split_axis=0, concat_axis=0, tiled=True)
    slots = lax.all_to_all(slot_voxels[0], ("gx", "gy"), split_axis=0, concat_axis=0, tiled=True)
    bricks_x, bricks_y, bricks_z = brick_mask.shape
    size_x, size_y, size_z = BRICK * bricks_x, BRICK * bricks_y, BRICK * bricks_z // 2
    features, channels = lift_weight.shape
    wide = down_leaf.shape[-1]
    rows_hi = size_x * size_y * size_z // 4
    span = 8 * features
    occ0 = spread(jnp.repeat(brick_mask, BRICK, 1), 1, BRICK // 2)
    occ1 = spread(brick_mask, BRICK // 2, BRICK // 2)
    occ2 = spread(brick_mask, BRICK // 4, BRICK // 4)
    occ3 = spread(brick_mask, 1, 1, 4)
    vmem = pl.BlockSpec(memory_space=pltpu.VMEM)
    leaf, top = pl.pallas_call(
        functools.partial(encoder, n_gx, n_gy),
        out_shape=(
            jax.ShapeDtypeStruct((size_x, size_y, size_z, 2 * channels), BF16),
            jax.ShapeDtypeStruct(occ3.shape, F32),
        ),
        in_specs=[vmem] * 11,
        out_specs=(vmem, vmem),
        scratch_shapes=[
            pltpu.VMEM((rows_hi, span), F32),
            pltpu.VMEM((size_x + 2, size_y + 2, size_z, 4 * channels), BF16),
            pltpu.VMEM((size_x + 2, size_y + 2, size_z, 4 * channels), BF16),
            pltpu.VMEM((size_x // 2 + 2, size_y // 2 + 2, size_z, wide), F32),
            pltpu.VMEM((size_x // 4 + 2, size_y // 4 + 2, size_z // 2, wide), F32),
            pltpu.VMEM((size_x // 8 + 2, size_y // 8 + 2, size_z // 2, wide), F32),
            pltpu.VMEM((size_x // 2 + 2, size_y // 2 + 2, size_z, 3 * wide), BF16),
            pltpu.VMEM((size_x // 2, size_y // 2, size_z, wide), F32),
            pltpu.VMEM((size_x // 4, size_y // 4, size_z, wide), F32),
            pltpu.SemaphoreType.DMA((5, 8)),
            pltpu.SemaphoreType.DMA((5, 8)),
        ],
        compiler_params=pltpu.CompilerParams(
            collective_id=0, has_side_effects=True, vmem_limit_bytes=56 * 1024 * 1024
        ),
        cost_estimate=pl.CostEstimate(
            flops=30_000_000_000, bytes_accessed=10_000_000, transcendentals=0
        ),
    )(
        arrived,
        slots,
        lift_blocks(lift_weight, 8),
        leaf_taps(leaf_convs),
        down_leaf.reshape(4, 2 * channels, wide),
        down_coarse.reshape(2, 8, wide, wide),
        coarse_convs.reshape(3, 9, 3 * wide, wide),
        occ0,
        occ1,
        occ2,
        occ3,
    )
    return leaf, top[:, :, :bricks_z].astype(BF16)


def solution(mesh):
    in_specs = (
        P(("gx", "gy"), None, None, None),
        P(("gx", "gy"), None, None),
        P("gx", "gy", None),
        P(),
        P(),
        P(),
        P(),
        P(),
    )
    out_specs = (P("gx", "gy", None, None), P("gx", "gy", None, None))
    return jax.shard_map(
        functools.partial(per_device, mesh.shape["gx"], mesh.shape["gy"]),
        mesh=mesh,
        in_specs=in_specs,
        out_specs=out_specs,
        check_vma=False,
    )
```

```python
import functools

import jax
import jax.numpy as jnp
from jax import lax
from jax.experimental import pallas as pl
from jax.experimental.pallas import tpu as pltpu
from jax.sharding import PartitionSpec as P

BRICK = 8
F32 = jnp.float32
BF16 = jnp.bfloat16
SIDES = [(-1, 0), (1, 0), (0, -1), (0, 1), (-1, -1), (-1, 1), (1, -1), (1, 1)]


def dot(left, right):
    return jnp.dot(left, right, preferred_element_type=F32)


def side_parts(count, here, other):
    near, far = 1, count
    own = {-1: near, 1: far, 0: pl.ds(1, count)}
    there = {-1: count + 1, 1: 0, 0: pl.ds(1, count)}
    return (own[here], own[other]), (there[here], there[other])


class Halo:
    def __init__(self, size_x, size_y, send_sems, recv_sems):
        self.place_x, self.place_y = lax.axis_index("gx"), lax.axis_index("gy")
        self.size_x, self.size_y = size_x, size_y
        self.send_sems, self.recv_sems = send_sems, recv_sems

    def each(self, action):
        for index, (step_x, step_y) in enumerate(SIDES):
            to_x, to_y = self.place_x + step_x, self.place_y + step_y
            tests = []
            if step_x:
                tests.append(to_x >= 0 if step_x < 0 else to_x < self.size_x)
            if step_y:
                tests.append(to_y >= 0 if step_y < 0 else to_y < self.size_y)
            exists = tests[0] if len(tests) == 1 else jnp.logical_and(*tests)

            @pl.when(exists)
            def _():
                action(index, step_x, step_y, (to_x, to_y))

    def copy(self, stage, buffer, index, step_x, step_y, target):
        source, landing = side_parts(buffer.shape[0] - 2, step_x, step_y)
        return pltpu.make_async_remote_copy(
            src_ref=buffer.at[source],
            dst_ref=buffer.at[landing],
            send_sem=self.send_sems.at[stage, index],
            recv_sem=self.recv_sems.at[stage, index],
            device_id=target,
            device_id_type=pl.DeviceIdType.MESH,
        )

    def start(self, stage, buffer):
        self.each(lambda *where: self.copy(stage, buffer, *where).start())

    def wait_arrived(self, stage, buffer):
        def arrived(index, step_x, step_y, target):
            opposite = SIDES.index((-step_x, -step_y))
            self.copy(stage, buffer, opposite, -step_x, -step_y, target).wait_recv()

        self.each(arrived)

    def wait_sent(self, stage, buffer):
        self.each(lambda *where: self.copy(stage, buffer, *where).wait_send())


def clear_border(buffer):
    last = buffer.shape[0] - 1
    edge = jnp.zeros(buffer.shape[1:], buffer.dtype)
    column = jnp.zeros((buffer.shape[0],) + buffer.shape[2:], buffer.dtype)
    buffer[0] = edge
    buffer[last] = edge
    buffer[:, 0] = column
    buffer[:, last] = column


def shift_rows(rows, period):
    count = rows.shape[0]
    z = lax.broadcasted_iota(jnp.int32, rows.shape, 0) % period
    before = jnp.where(z == 0, 0.0, pltpu.roll(rows, 1, 0))
    after = jnp.where(z == period - 1, 0.0, pltpu.roll(rows, count - 1, 0))
    return before, after


def store_leaf(buffer, at_x, at_y, rows, shape):
    before, after = shift_rows(rows, shape[2])
    lane = lax.broadcasted_iota(jnp.int32, rows.shape, 1)
    outer = jnp.where(lane < rows.shape[1] // 2, after, before)
    both = jnp.concatenate([rows, outer], -1).astype(BF16)
    buffer[at_x, at_y] = both.reshape(shape[:3] + (both.shape[-1],))


def stacked_z(values):
    shape = values.shape
    rows = values.reshape(-1, shape[-1])
    before, after = shift_rows(rows, shape[2])
    return jnp.concatenate([before, rows, after], -1).reshape(shape[:3] + (3 * shape[3],))


def pair_part(values, part_x, part_y):
    size_x, size_y = values.shape[:2]
    split = values.reshape((size_x // 2, 2, size_y // 2, 2) + values.shape[2:])
    return split[:, part_x, :, part_y]


def encoder(
    n_gx,
    n_gy,
    records,
    slots,
    lift_weight,
    leaf_convs,
    down_leaf,
    down_coarse_far,
    coarse_convs_far,
    occupied,
    leaf_out,
    top_out,
    arrived,
    slots_out,
    slots_in,
    taps,
    down_coarse,
    coarse_convs,
    summed,
    leaf_a,
    leaf_b,
    coarse_a,
    coarse_b,
    coarse_c,
    stacked,
    level_one,
    level_two,
    send_sems,
    recv_sems,
    owner_send_sems,
    owner_recv_sems,
    local_sems,
):
    halo = Halo(n_gx, n_gy, send_sems, recv_sems)
    senders = n_gx * n_gy
    me = halo.place_x * n_gy + halo.place_y
    weights = (
        pltpu.make_async_copy(down_coarse_far, down_coarse, local_sems.at[0]),
        pltpu.make_async_copy(coarse_convs_far, coarse_convs, local_sems.at[1]),
    )
    own_records = pltpu.make_async_copy(records.at[me], arrived.at[0], local_sems.at[2])
    own_records.start()

    def owner(away):
        index = lax.rem(me + away, senders)
        return index, (index // n_gy, lax.rem(index, n_gy))

    barrier = pltpu.get_barrier_semaphore()

    def greet(away, carry):
        pl.semaphore_signal(
            barrier, inc=1, device_id=owner(away)[1], device_id_type=pl.DeviceIdType.MESH
        )
        return carry

    for buffer in (leaf_a, leaf_b, coarse_a, coarse_b, coarse_c):
        clear_border(buffer)
    lax.fori_loop(1, senders, greet, 0)

    def stage_slots(step, carry):
        base = pl.multiple_of(step * 8, 8)
        index = slots[pl.ds(base, 8), :]
        for place in range(8):
            slots_out[base + place] = index[place : place + 1]
        return carry

    lax.fori_loop(0, senders // 8, stage_slots, 0)
    slots_in[0] = slots_out[me]
    pl.semaphore_wait(barrier, senders - 1)

    def owner_copies(away):
        index, target = owner(away)
        return (
            pltpu.make_async_remote_copy(
                src_ref=slots_out.at[index],
                dst_ref=slots_in.at[away],
                send_sem=owner_send_sems.at[0, away],
                recv_sem=owner_recv_sems.at[0, away],
                device_id=target,
                device_id_type=pl.DeviceIdType.MESH,
            ),
            pltpu.make_async_remote_copy(
                src_ref=records.at[index],
                dst_ref=arrived.at[away],
                send_sem=owner_send_sems.at[1, away],
                recv_sem=owner_recv_sems.at[1, away],
                device_id=target,
                device_id_type=pl.DeviceIdType.MESH,
            ),
        )

    def send_owner(away, carry):
        for copy in owner_copies(away):
            copy.start()
        return carry

    def owner_arrived(away, carry):
        for copy in owner_copies(away):
            copy.wait_recv()
        return carry

    def owner_sent(away, carry):
        for copy in owner_copies(away):
            copy.wait_send()
        return carry

    lax.fori_loop(1, senders, send_owner, 0)
    for copy in weights:
        copy.start()

    for layer in range(2):
        for step in range(9):
            low, mid, high = (leaf_convs[layer, step, tap] for tap in range(3))
            none = jnp.zeros_like(low)
            first = jnp.concatenate([mid, high, none, low], 0)
            second = jnp.concatenate([low, mid, high, none], 0)
            taps[layer, step] = jnp.concatenate([first, second], 1)

    slot_rows, width = arrived.shape[1:]
    cap = slots.shape[1]
    lanes = cap // slot_rows
    features = width // lanes
    span = summed.shape[1]
    rows_hi = summed.shape[0]
    group = 4
    order_from = lax.broadcasted_iota(jnp.int32, (cap, cap), 0)
    order_to = lax.broadcasted_iota(jnp.int32, (cap, cap), 1)
    order = jnp.where(
        order_from == (order_to % slot_rows) * lanes + order_to // slot_rows, 1.0, 0.0
    ).astype(BF16)
    pick_from = lax.broadcasted_iota(jnp.int32, (width, lanes * span), 0)
    pick_to = lax.broadcasted_iota(jnp.int32, (width, lanes * span), 1)
    pick = jnp.where(
        pick_from == (pick_to // span) * features + pick_to % features, 1.0, 0.0
    ).astype(BF16)
    column_group = (
        lax.broadcasted_iota(jnp.int32, (cap, span), 1) // features
    ).astype(F32)
    row_index = lax.broadcasted_iota(jnp.int32, (rows_hi, cap), 0).astype(F32)
    summed[...] = jnp.zeros_like(summed)

    def add_group(step, carry):
        base = step * 8
        lax.fori_loop(jnp.where(step > 0, base, 1), base + 8, owner_arrived, 0)
        index = jnp.concatenate([slots_in[base + place] for place in range(8)], 0)
        wide_all = dot(arrived[pl.ds(base, 8)].reshape(8 * slot_rows, width), pick)
        half = index // 2
        high = half % rows_hi
        low = (index // (2 * rows_hi)) * 2 + index % 2
        high_row = 64.0 * dot((high // 64).astype(F32).astype(BF16), order) + dot(
            (high % 64).astype(F32).astype(BF16), order
        )
        low_column = lax.dot_general(
            order,
            low.astype(F32).astype(BF16),
            (((0,), (1,)), ((), ())),
            preferred_element_type=F32,
        )
        for part in range(8 // group):
            hots, tables = [], []
            for inner in range(group):
                place = part * group + inner
                hot = jnp.where(row_index == high_row[place : place + 1], 1.0, 0.0)
                hots.append(hot.astype(BF16))
                wide = wide_all[place * slot_rows : (place + 1) * slot_rows]
                wide = jnp.concatenate(
                    [wide[:, lane * span : (lane + 1) * span] for lane in range(lanes)], 0
                )
                tables.append(
                    jnp.where(column_group == low_column[:, place : place + 1], wide, 0.0).astype(
                        BF16
                    )
                )
            summed[...] += dot(jnp.concatenate(hots, 1), jnp.concatenate(tables, 0))
        return carry

    own_records.wait()
    lax.fori_loop(0, senders // 8, add_group, 0)

    size_x, size_y, size_z, leaf_width = leaf_out.shape
    quarter = rows_hi // (size_y * size_z)
    channels = lift_weight.shape[1]
    lift_shape = (span, span // features * channels)
    copy_rows = (
        lax.broadcasted_iota(jnp.int32, (span, features), 0) % features
        == lax.broadcasted_iota(jnp.int32, (span, features), 1)
    )
    copy_columns = (
        lax.broadcasted_iota(jnp.int32, (channels, lift_shape[1]), 1) % channels
        == lax.broadcasted_iota(jnp.int32, (channels, lift_shape[1]), 0)
    )
    lift = dot(jnp.where(copy_rows, 1.0, 0.0).astype(BF16), lift_weight[...])
    lift = dot(lift.astype(BF16), jnp.where(copy_columns, 1.0, 0.0).astype(BF16))
    on_block = (
        lax.broadcasted_iota(jnp.int32, lift_shape, 0) // features
        == lax.broadcasted_iota(jnp.int32, lift_shape, 1) // channels
    )
    lift = jnp.where(on_block, lift, 0.0).astype(BF16)
    rest = summed[...]
    lifted = 0.0
    for piece in range(3):
        cut = rest.astype(BF16)
        rest = rest - cut.astype(F32)
        lifted = lifted + dot(cut, lift)
    inside_y = pl.ds(1, size_y)
    for block in range(size_x // quarter):
        store_leaf(
            leaf_a,
            pl.ds(1 + block * quarter, quarter),
            inside_y,
            lifted[:, block * leaf_width : (block + 1) * leaf_width],
            (quarter, size_y, size_z),
        )

    halo.start(0, leaf_a)

    def convolve(source, layer, x, count_x, y, count_y):
        total = None
        for step in range(9):
            window = source[pl.ds(x + step // 3, count_x), pl.ds(y + step % 3, count_y)]
            term = dot(window.reshape(-1, window.shape[-1]), taps[layer, step])
            total = term if total is None else total + term
        return jnp.maximum(total, 0.0)

    def leaf_layer(source, layer, emit):
        def block(x, count_x, y, count_y):
            swept = convolve(source, layer, x, count_x, y, count_y)
            mask = jnp.concatenate(
                [
                    occupied[(x + step_x) // BRICK, (y + step_y) // BRICK, 0:size_z]
                    for step_x in range(count_x)
                    for step_y in range(count_y)
                ],
                0,
            )
            emit(x, count_x, y, count_y, swept * mask)

        def inner(step, carry):
            block(1 + 2 * step, 2, 1, size_y - 2)
            return carry

        lax.fori_loop(0, (size_x - 2) // 2, inner, 0)
        halo.wait_arrived(layer, source)
        block(0, 1, 0, size_y)
        block(size_x - 1, 1, 0, size_y)
        block(1, size_x - 2, 0, 1)
        block(1, size_x - 2, size_y - 1, 1)

    def keep_first(x, count_x, y, count_y, rows):
        store_leaf(
            leaf_b,
            pl.ds(1 + x, count_x),
            pl.ds(1 + y, count_y),
            rows,
            (count_x, count_y, size_z),
        )

    def keep_second(x, count_x, y, count_y, rows):
        leaf_out[pl.ds(x, count_x), pl.ds(y, count_y)] = rows.astype(BF16).reshape(
            count_x, count_y, size_z, leaf_width
        )

    leaf_layer(leaf_a, 0, keep_first)
    halo.start(1, leaf_b)
    leaf_layer(leaf_b, 1, keep_second)

    def widen(mask, factor):
        size = mask.shape[0] * factor
        return jnp.stack(
            [
                jnp.stack([mask[x // factor, y // factor] for y in range(size)])
                for x in range(size)
            ]
        )

    occ1 = widen(occupied[:, :, 0:size_z], BRICK // 2)
    occ2 = widen(occupied[:, :, pl.ds(0, size_z // 2, 2)], BRICK // 4)
    occ3 = occupied[:, :, size_z : size_z + size_z // 2]

    def coarse_conv(level, kernel, occupied):
        count, depth = kernel.shape[0] - 2, kernel.shape[2]
        total = None
        for step in range(9):
            step_x, step_y = step // 3, step % 3
            window = kernel[step_x : step_x + count, step_y : step_y + count]
            window = window.reshape(count * count * depth, window.shape[-1]).astype(BF16)
            term = dot(window, coarse_convs[level, step])
            total = term if total is None else total + term
        return jnp.maximum(total, 0.0).reshape(occupied.shape) * occupied

    def finish_down(stage, buffer, total, occupied):
        count = occupied.shape[0]
        cells = jnp.maximum(total, 0.0).reshape(occupied.shape) * occupied
        buffer[1 : count + 1, 1 : count + 1] = cells
        halo.start(stage, buffer)
        halo.wait_arrived(stage, buffer)

    for copy in weights:
        copy.wait()
    total = 0.0
    leaf = leaf_out[...]
    for part in range(4):
        piece = pair_part(leaf, part // 2, part % 2)
        total = total + dot(piece.reshape(-1, leaf_width), down_leaf[part])
    finish_down(2, coarse_a, total, occ1)
    stacked[...] = stacked_z(coarse_a[...]).astype(BF16)
    level_one[...] = coarse_conv(0, stacked, occ1)

    def shrink(level, source, depth):
        total = 0.0
        for part_z in range(2):
            half = source[:, :, pl.ds(part_z, depth, 2), :]
            for part in range(4):
                piece = pair_part(half, part // 2, part % 2)
                piece = piece.reshape(-1, piece.shape[-1]).astype(BF16)
                total = total + dot(piece, down_coarse[level, 2 * part + part_z])
        return total

    finish_down(3, coarse_b, shrink(0, level_one, occ2.shape[2]), occ2)
    deep = occ2.shape[2]
    level_two[:, :, deep : 2 * deep] = jnp.zeros_like(occ2)
    level_two[:, :, 0:deep] = coarse_conv(1, stacked_z(coarse_b[...]), occ2)
    finish_down(4, coarse_c, shrink(1, level_two, occ3.shape[2]), occ3)
    top = coarse_conv(2, stacked_z(coarse_c[...]), occ3)
    top_out[...] = top[:, :, 0 : top_out.shape[2]].astype(BF16)
    lax.fori_loop(1, senders, owner_sent, 0)

    for stage, buffer in enumerate((leaf_a, leaf_b, coarse_a, coarse_b, coarse_c)):
        halo.wait_sent(stage, buffer)


def per_device(
    n_gx,
    n_gy,
    records,
    slot_voxels,
    brick_mask,
    lift_weight,
    leaf_convs,
    down_leaf,
    down_coarse,
    coarse_convs,
):
    bricks_x, bricks_y, bricks_z = brick_mask.shape
    size_x, size_y, size_z = BRICK * bricks_x, BRICK * bricks_y, BRICK * bricks_z // 2
    features, channels = lift_weight.shape
    wide = down_leaf.shape[-1]
    rows_hi = size_x * size_y * size_z // 4
    span = 8 * features
    senders, slot_rows, width = records.shape[1:]
    cap = slot_voxels.shape[-1]
    fine = jnp.repeat(brick_mask, BRICK // 2, 2)
    padding = ((0, 0), (0, 0), (0, size_z // 2 - bricks_z))
    mask = jnp.concatenate([fine, jnp.pad(brick_mask, padding)], 2).astype(F32)
    mask = jnp.broadcast_to(mask[..., None], mask.shape + (2 * channels,))
    far = pl.BlockSpec(memory_space=pl.ANY)
    vmem = pl.BlockSpec(memory_space=pltpu.VMEM)
    leaf, top = pl.pallas_call(
        functools.partial(encoder, n_gx, n_gy),
        out_shape=(
            jax.ShapeDtypeStruct((size_x, size_y, size_z, 2 * channels), BF16),
            jax.ShapeDtypeStruct((bricks_x, bricks_y, bricks_z, wide), BF16),
        ),
        in_specs=[far, vmem, vmem, vmem, vmem, far, far, vmem],
        out_specs=(vmem, vmem),
        scratch_shapes=[
            pltpu.VMEM((senders, slot_rows, width), BF16),
            pltpu.VMEM((senders, 1, cap), jnp.int32),
            pltpu.VMEM((senders, 1, cap), jnp.int32),
            pltpu.VMEM((2, 9, 4 * channels, 2 * channels), BF16),
            pltpu.VMEM((2, 8, wide, wide), BF16),
            pltpu.VMEM((3, 9, 3 * wide, wide), BF16),
            pltpu.VMEM((rows_hi, span), F32),
            pltpu.VMEM((size_x + 2, size_y + 2, size_z, 4 * channels), BF16),
            pltpu.VMEM((size_x + 2, size_y + 2, size_z, 4 * channels), BF16),
            pltpu.VMEM((size_x // 2 + 2, size_y // 2 + 2, size_z, wide), F32),
            pltpu.VMEM((size_x // 4 + 2, size_y // 4 + 2, size_z // 2, wide), F32),
            pltpu.VMEM((size_x // 8 + 2, size_y // 8 + 2, size_z // 2, wide), F32),
            pltpu.VMEM((size_x // 2 + 2, size_y // 2 + 2, size_z, 3 * wide), BF16),
            pltpu.VMEM((size_x // 2, size_y // 2, size_z, wide), F32),
            pltpu.VMEM((size_x // 4, size_y // 4, size_z, wide), F32),
            pltpu.SemaphoreType.DMA((5, 8)),
            pltpu.SemaphoreType.DMA((5, 8)),
            pltpu.SemaphoreType.DMA((2, senders)),
            pltpu.SemaphoreType.DMA((2, senders)),
            pltpu.SemaphoreType.DMA((3,)),
        ],
        compiler_params=pltpu.CompilerParams(
            collective_id=0, has_side_effects=True, vmem_limit_bytes=56 * 1024 * 1024
        ),
        cost_estimate=pl.CostEstimate(
            flops=30_000_000_000, bytes_accessed=10_000_000, transcendentals=0
        ),
    )(
        records[0],
        slot_voxels[0],
        lift_weight,
        leaf_convs.reshape(2, 9, 3, channels, channels),
        down_leaf.reshape(4, 2 * channels, wide),
        down_coarse.reshape(2, 8, wide, wide),
        coarse_convs.reshape(3, 9, 3 * wide, wide),
        mask,
    )
    return leaf, top


def solution(mesh):
    in_specs = (
        P(("gx", "gy"), None, None, None),
        P(("gx", "gy"), None, None),
        P("gx", "gy", None),
        P(),
        P(),
        P(),
        P(),
        P(),
    )
    out_specs = (P("gx", "gy", None, None), P("gx", "gy", None, None))
    return jax.shard_map(
        functools.partial(per_device, mesh.shape["gx"], mesh.shape["gy"]),
        mesh=mesh,
        in_specs=in_specs,
        out_specs=out_specs,
        check_vma=False,
    )
```

```python
import functools

import jax
import jax.numpy as jnp
from jax import lax
from jax.experimental import pallas as pl
from jax.experimental.pallas import tpu as pltpu
from jax.sharding import PartitionSpec as P

BRICK = 8
F32 = jnp.float32
BF16 = jnp.bfloat16
SIDES = [(-1, 0), (1, 0), (0, -1), (0, 1), (-1, -1), (-1, 1), (1, -1), (1, 1)]


def dot(left, right):
    return jnp.dot(left, right, preferred_element_type=F32)


def over(value, size):
    if size & (size - 1):
        return value // size
    return lax.shift_right_logical(value, jnp.full_like(value, size.bit_length() - 1))


def within(value, size):
    return value % size if size & (size - 1) else value & (size - 1)


def side_parts(count, here, other):
    near, far = 1, count
    own = {-1: near, 1: far, 0: pl.ds(1, count)}
    there = {-1: count + 1, 1: 0, 0: pl.ds(1, count)}
    return (own[here], own[other]), (there[here], there[other])


class Halo:
    def __init__(self, size_x, size_y, send_sems, recv_sems):
        self.place_x, self.place_y = lax.axis_index("gx"), lax.axis_index("gy")
        self.size_x, self.size_y = size_x, size_y
        self.send_sems, self.recv_sems = send_sems, recv_sems

    def each(self, action):
        for index, (step_x, step_y) in enumerate(SIDES):
            to_x, to_y = self.place_x + step_x, self.place_y + step_y
            tests = []
            if step_x:
                tests.append(to_x >= 0 if step_x < 0 else to_x < self.size_x)
            if step_y:
                tests.append(to_y >= 0 if step_y < 0 else to_y < self.size_y)
            exists = tests[0] if len(tests) == 1 else jnp.logical_and(*tests)

            @pl.when(exists)
            def _():
                action(index, step_x, step_y, (to_x, to_y))

    def copy(self, stage, buffer, index, step_x, step_y, target):
        source, landing = side_parts(buffer.shape[0] - 2, step_x, step_y)
        return pltpu.make_async_remote_copy(
            src_ref=buffer.at[source],
            dst_ref=buffer.at[landing],
            send_sem=self.send_sems.at[stage, index],
            recv_sem=self.recv_sems.at[stage, index],
            device_id=target,
            device_id_type=pl.DeviceIdType.MESH,
        )

    def start(self, stage, buffer):
        self.each(lambda *where: self.copy(stage, buffer, *where).start())

    def wait_arrived(self, stage, buffer):
        def arrived(index, step_x, step_y, target):
            opposite = SIDES.index((-step_x, -step_y))
            self.copy(stage, buffer, opposite, -step_x, -step_y, target).wait_recv()

        self.each(arrived)

    def wait_sent(self, stage, buffer):
        self.each(lambda *where: self.copy(stage, buffer, *where).wait_send())


def clear_border(buffer):
    last = buffer.shape[0] - 1
    edge = jnp.zeros(buffer.shape[1:], buffer.dtype)
    column = jnp.zeros((buffer.shape[0],) + buffer.shape[2:], buffer.dtype)
    buffer[0] = edge
    buffer[last] = edge
    buffer[:, 0] = column
    buffer[:, last] = column


def shift_rows(rows, period):
    count = rows.shape[0]
    z = within(lax.broadcasted_iota(jnp.int32, rows.shape, 0), period)
    before = jnp.where(z == 0, 0.0, pltpu.roll(rows, 1, 0))
    after = jnp.where(z == period - 1, 0.0, pltpu.roll(rows, count - 1, 0))
    return before, after


def store_leaf(buffer, at_x, at_y, rows, shape):
    before, after = shift_rows(rows, shape[2])
    lane = lax.broadcasted_iota(jnp.int32, rows.shape, 1)
    outer = jnp.where(lane < rows.shape[1] // 2, after, before)
    both = jnp.concatenate([rows, outer], -1).astype(BF16)
    buffer[at_x, at_y] = both.reshape(shape[:3] + (both.shape[-1],))


def stacked_z(values):
    shape = values.shape
    rows = values.reshape(-1, shape[-1])
    before, after = shift_rows(rows, shape[2])
    return jnp.concatenate([before, rows, after], -1).reshape(shape[:3] + (3 * shape[3],))


def pair_part(values, part_x, part_y):
    size_x, size_y = values.shape[:2]
    split = values.reshape((size_x // 2, 2, size_y // 2, 2) + values.shape[2:])
    return split[:, part_x, :, part_y]


def encoder(
    n_gx,
    n_gy,
    records,
    slots,
    lift_weight,
    leaf_convs,
    down_leaf,
    down_coarse_far,
    coarse_convs_far,
    brick_mask,
    leaf_out,
    top_out,
    occupied,
    arrived,
    slots_out,
    slots_in,
    taps,
    down_coarse,
    coarse_convs,
    summed,
    leaf_a,
    leaf_b,
    coarse_a,
    coarse_b,
    coarse_c,
    stacked,
    level_one,
    level_two,
    send_sems,
    recv_sems,
    owner_send_sems,
    owner_recv_sems,
    local_sems,
):
    halo = Halo(n_gx, n_gy, send_sems, recv_sems)
    senders = n_gx * n_gy
    me = halo.place_x * n_gy + halo.place_y
    weights = (
        pltpu.make_async_copy(down_coarse_far, down_coarse, local_sems.at[0]),
        pltpu.make_async_copy(coarse_convs_far, coarse_convs, local_sems.at[1]),
    )
    own_records = pltpu.make_async_copy(records.at[me], arrived.at[0], local_sems.at[2])
    own_records.start()

    def owner(away):
        index = lax.rem(me + away, senders)
        return index, (index // n_gy, lax.rem(index, n_gy))

    barrier = pltpu.get_barrier_semaphore()

    def greet(away, carry):
        pl.semaphore_signal(
            barrier, inc=1, device_id=owner(away)[1], device_id_type=pl.DeviceIdType.MESH
        )
        return carry

    for buffer in (leaf_a, leaf_b, coarse_a, coarse_b, coarse_c):
        clear_border(buffer)
    lax.fori_loop(1, senders, greet, 0)

    def stage_slots(step, carry):
        base = pl.multiple_of(step * 8, 8)
        index = slots[pl.ds(base, 8), :]
        for place in range(8):
            slots_out[base + place] = index[place : place + 1]
        return carry

    lax.fori_loop(0, senders // 8, stage_slots, 0)
    slots_in[0] = slots_out[me]
    pl.semaphore_wait(barrier, senders - 1)

    def owner_copies(away):
        index, target = owner(away)
        return (
            pltpu.make_async_remote_copy(
                src_ref=slots_out.at[index],
                dst_ref=slots_in.at[away],
                send_sem=owner_send_sems.at[0, away],
                recv_sem=owner_recv_sems.at[0, away],
                device_id=target,
                device_id_type=pl.DeviceIdType.MESH,
            ),
            pltpu.make_async_remote_copy(
                src_ref=records.at[index],
                dst_ref=arrived.at[away],
                send_sem=owner_send_sems.at[1, away],
                recv_sem=owner_recv_sems.at[1, away],
                device_id=target,
                device_id_type=pl.DeviceIdType.MESH,
            ),
        )

    def send_owner(away, carry):
        for copy in owner_copies(away):
            copy.start()
        return carry

    def owner_arrived(away, carry):
        for copy in owner_copies(away):
            copy.wait_recv()
        return carry

    def owner_sent(away, carry):
        for copy in owner_copies(away):
            copy.wait_send()
        return carry

    lax.fori_loop(1, senders, send_owner, 0)
    for copy in weights:
        copy.start()

    bricks_x, bricks_y, bricks_z = brick_mask.shape
    mask_rows, fine_rows = occupied.shape[2], leaf_out.shape[2]
    row = lax.broadcasted_iota(jnp.int32, (mask_rows, bricks_z), 0)
    brick = jnp.where(row < fine_rows, over(row, BRICK // 2), row - fine_rows)
    here = brick == lax.broadcasted_iota(jnp.int32, (mask_rows, bricks_z), 1)
    for brick_x in range(bricks_x):
        for brick_y in range(bricks_y):
            line = brick_mask[brick_x, brick_y : brick_y + 1, :].astype(F32)
            line = jnp.sum(jnp.where(here, line, 0.0), axis=1, keepdims=True)
            occupied[brick_x, brick_y] = jnp.broadcast_to(line, occupied.shape[2:])

    for layer in range(2):
        for step in range(9):
            low, mid, high = (leaf_convs[layer, step, tap] for tap in range(3))
            none = jnp.zeros_like(low)
            first = jnp.concatenate([mid, high, none, low], 0)
            second = jnp.concatenate([low, mid, high, none], 0)
            taps[layer, step] = jnp.concatenate([first, second], 1)

    slot_rows, width = arrived.shape[1:]
    cap = slots.shape[1]
    lanes = cap // slot_rows
    features = width // lanes
    span = summed.shape[1]
    rows_hi = summed.shape[0]
    group = 4
    order_from = lax.broadcasted_iota(jnp.int32, (cap, cap), 0)
    order_to = lax.broadcasted_iota(jnp.int32, (cap, cap), 1)
    order = jnp.where(
        order_from == within(order_to, slot_rows) * lanes + over(order_to, slot_rows), 1.0, 0.0
    ).astype(BF16)
    pick_from = lax.broadcasted_iota(jnp.int32, (width, lanes * span), 0)
    pick_to = lax.broadcasted_iota(jnp.int32, (width, lanes * span), 1)
    pick = jnp.where(
        pick_from == over(pick_to, span) * features + within(pick_to, features), 1.0, 0.0
    ).astype(BF16)
    column_group = over(lax.broadcasted_iota(jnp.int32, (cap, span), 1), features).astype(F32)
    row_index = lax.broadcasted_iota(jnp.int32, (rows_hi, cap), 0).astype(F32)
    summed[...] = jnp.zeros_like(summed)

    def add_group(step, carry):
        base = step * 8
        lax.fori_loop(jnp.where(step > 0, base, 1), base + 8, owner_arrived, 0)
        index = jnp.concatenate([slots_in[base + place] for place in range(8)], 0)
        wide_all = dot(arrived[pl.ds(base, 8)].reshape(8 * slot_rows, width), pick)
        high = within(over(index, 2), rows_hi)
        low = over(index, 2 * rows_hi) * 2 + within(index, 2)
        high_row = 64.0 * dot(over(high, 64).astype(F32).astype(BF16), order) + dot(
            within(high, 64).astype(F32).astype(BF16), order
        )
        low_column = lax.dot_general(
            order,
            low.astype(F32).astype(BF16),
            (((0,), (1,)), ((), ())),
            preferred_element_type=F32,
        )
        for part in range(8 // group):
            hots, tables = [], []
            for inner in range(group):
                place = part * group + inner
                hot = jnp.where(row_index == high_row[place : place + 1], 1.0, 0.0)
                hots.append(hot.astype(BF16))
                wide = wide_all[place * slot_rows : (place + 1) * slot_rows]
                wide = jnp.concatenate(
                    [wide[:, lane * span : (lane + 1) * span] for lane in range(lanes)], 0
                )
                tables.append(
                    jnp.where(column_group == low_column[:, place : place + 1], wide, 0.0).astype(
                        BF16
                    )
                )
            summed[...] += dot(jnp.concatenate(hots, 1), jnp.concatenate(tables, 0))
        return carry

    own_records.wait()
    lax.fori_loop(0, senders // 8, add_group, 0)

    size_x, size_y, size_z, leaf_width = leaf_out.shape
    quarter = rows_hi // (size_y * size_z)
    channels = lift_weight.shape[1]
    lift_shape = (span, span // features * channels)
    copy_rows = (
        within(lax.broadcasted_iota(jnp.int32, (span, features), 0), features)
        == lax.broadcasted_iota(jnp.int32, (span, features), 1)
    )
    copy_columns = (
        within(lax.broadcasted_iota(jnp.int32, (channels, lift_shape[1]), 1), channels)
        == lax.broadcasted_iota(jnp.int32, (channels, lift_shape[1]), 0)
    )
    lift = dot(jnp.where(copy_rows, 1.0, 0.0).astype(BF16), lift_weight[...])
    lift = dot(lift.astype(BF16), jnp.where(copy_columns, 1.0, 0.0).astype(BF16))
    on_block = (
        over(lax.broadcasted_iota(jnp.int32, lift_shape, 0), features)
        == over(lax.broadcasted_iota(jnp.int32, lift_shape, 1), channels)
    )
    lift = jnp.where(on_block, lift, 0.0).astype(BF16)
    rest = summed[...]
    lifted = 0.0
    for piece in range(3):
        cut = rest.astype(BF16)
        rest = rest - cut.astype(F32)
        lifted = lifted + dot(cut, lift)
    inside_y = pl.ds(1, size_y)
    for block in range(size_x // quarter):
        store_leaf(
            leaf_a,
            pl.ds(1 + block * quarter, quarter),
            inside_y,
            lifted[:, block * leaf_width : (block + 1) * leaf_width],
            (quarter, size_y, size_z),
        )

    halo.start(0, leaf_a)

    def convolve(source, layer, x, count_x, y, count_y):
        total = None
        for step in range(9):
            window = source[pl.ds(x + step // 3, count_x), pl.ds(y + step % 3, count_y)]
            term = dot(window.reshape(-1, window.shape[-1]), taps[layer, step])
            total = term if total is None else total + term
        return jnp.maximum(total, 0.0)

    def leaf_layer(source, layer, emit):
        def block(x, count_x, y, count_y):
            swept = convolve(source, layer, x, count_x, y, count_y)
            mask = jnp.concatenate(
                [
                    occupied[(x + step_x) // BRICK, (y + step_y) // BRICK, 0:size_z]
                    for step_x in range(count_x)
                    for step_y in range(count_y)
                ],
                0,
            )
            emit(x, count_x, y, count_y, swept * mask)

        def inner(step, carry):
            block(1 + 2 * step, 2, 1, size_y - 2)
            return carry

        lax.fori_loop(0, (size_x - 2) // 2, inner, 0)
        halo.wait_arrived(layer, source)
        block(0, 1, 0, size_y)
        block(size_x - 1, 1, 0, size_y)
        block(1, size_x - 2, 0, 1)
        block(1, size_x - 2, size_y - 1, 1)

    def keep_first(x, count_x, y, count_y, rows):
        store_leaf(
            leaf_b,
            pl.ds(1 + x, count_x),
            pl.ds(1 + y, count_y),
            rows,
            (count_x, count_y, size_z),
        )

    def keep_second(x, count_x, y, count_y, rows):
        leaf_out[pl.ds(x, count_x), pl.ds(y, count_y)] = rows.astype(BF16).reshape(
            count_x, count_y, size_z, leaf_width
        )

    leaf_layer(leaf_a, 0, keep_first)
    halo.start(1, leaf_b)
    leaf_layer(leaf_b, 1, keep_second)

    def widen(mask, factor):
        size = mask.shape[0] * factor
        return jnp.stack(
            [
                jnp.stack([mask[x // factor, y // factor] for y in range(size)])
                for x in range(size)
            ]
        )

    occ1 = widen(occupied[:, :, 0:size_z], BRICK // 2)
    occ2 = widen(occupied[:, :, pl.ds(0, size_z // 2, 2)], BRICK // 4)
    occ3 = occupied[:, :, size_z : size_z + size_z // 2]

    def coarse_conv(level, kernel, occupied):
        count, depth = kernel.shape[0] - 2, kernel.shape[2]
        total = None
        for step in range(9):
            step_x, step_y = step // 3, step % 3
            window = kernel[step_x : step_x + count, step_y : step_y + count]
            window = window.reshape(count * count * depth, window.shape[-1]).astype(BF16)
            term = dot(window, coarse_convs[level, step])
            total = term if total is None else total + term
        return jnp.maximum(total, 0.0).reshape(occupied.shape) * occupied

    def finish_down(stage, buffer, total, occupied):
        count = occupied.shape[0]
        cells = jnp.maximum(total, 0.0).reshape(occupied.shape) * occupied
        buffer[1 : count + 1, 1 : count + 1] = cells
        halo.start(stage, buffer)
        halo.wait_arrived(stage, buffer)

    for copy in weights:
        copy.wait()
    total = 0.0
    leaf = leaf_out[...]
    for part in range(4):
        piece = pair_part(leaf, part // 2, part % 2)
        total = total + dot(piece.reshape(-1, leaf_width), down_leaf[part])
    finish_down(2, coarse_a, total, occ1)
    stacked[...] = stacked_z(coarse_a[...]).astype(BF16)
    level_one[...] = coarse_conv(0, stacked, occ1)

    def shrink(level, source, depth):
        total = 0.0
        for part_z in range(2):
            half = source[:, :, pl.ds(part_z, depth, 2), :]
            for part in range(4):
                piece = pair_part(half, part // 2, part % 2)
                piece = piece.reshape(-1, piece.shape[-1]).astype(BF16)
                total = total + dot(piece, down_coarse[level, 2 * part + part_z])
        return total

    finish_down(3, coarse_b, shrink(0, level_one, occ2.shape[2]), occ2)
    deep = occ2.shape[2]
    level_two[:, :, deep : 2 * deep] = jnp.zeros_like(occ2)
    level_two[:, :, 0:deep] = coarse_conv(1, stacked_z(coarse_b[...]), occ2)
    finish_down(4, coarse_c, shrink(1, level_two, occ3.shape[2]), occ3)
    top = coarse_conv(2, stacked_z(coarse_c[...]), occ3)
    top_out[...] = top[:, :, 0 : top_out.shape[2]].astype(BF16)
    lax.fori_loop(1, senders, owner_sent, 0)

    for stage, buffer in enumerate((leaf_a, leaf_b, coarse_a, coarse_b, coarse_c)):
        halo.wait_sent(stage, buffer)


def per_device(
    n_gx,
    n_gy,
    records,
    slot_voxels,
    brick_mask,
    lift_weight,
    leaf_convs,
    down_leaf,
    down_coarse,
    coarse_convs,
):
    bricks_x, bricks_y, bricks_z = brick_mask.shape
    size_x, size_y, size_z = BRICK * bricks_x, BRICK * bricks_y, BRICK * bricks_z // 2
    features, channels = lift_weight.shape
    wide = down_leaf.shape[-1]
    rows_hi = size_x * size_y * size_z // 4
    span = 8 * features
    senders, slot_rows, width = records.shape[1:]
    cap = slot_voxels.shape[-1]
    far = pl.BlockSpec(memory_space=pl.ANY)
    vmem = pl.BlockSpec(memory_space=pltpu.VMEM)
    leaf, top = pl.pallas_call(
        functools.partial(encoder, n_gx, n_gy),
        out_shape=(
            jax.ShapeDtypeStruct((size_x, size_y, size_z, 2 * channels), BF16),
            jax.ShapeDtypeStruct((bricks_x, bricks_y, bricks_z, wide), BF16),
        ),
        in_specs=[far, vmem, vmem, vmem, vmem, far, far, vmem],
        out_specs=(vmem, vmem),
        scratch_shapes=[
            pltpu.VMEM((bricks_x, bricks_y, size_z + size_z // 2, 2 * channels), F32),
            pltpu.VMEM((senders, slot_rows, width), BF16),
            pltpu.VMEM((senders, 1, cap), jnp.int32),
            pltpu.VMEM((senders, 1, cap), jnp.int32),
            pltpu.VMEM((2, 9, 4 * channels, 2 * channels), BF16),
            pltpu.VMEM((2, 8, wide, wide), BF16),
            pltpu.VMEM((3, 9, 3 * wide, wide), BF16),
            pltpu.VMEM((rows_hi, span), F32),
            pltpu.VMEM((size_x + 2, size_y + 2, size_z, 4 * channels), BF16),
            pltpu.VMEM((size_x + 2, size_y + 2, size_z, 4 * channels), BF16),
            pltpu.VMEM((size_x // 2 + 2, size_y // 2 + 2, size_z, wide), F32),
            pltpu.VMEM((size_x // 4 + 2, size_y // 4 + 2, size_z // 2, wide), F32),
            pltpu.VMEM((size_x // 8 + 2, size_y // 8 + 2, size_z // 2, wide), F32),
            pltpu.VMEM((size_x // 2 + 2, size_y // 2 + 2, size_z, 3 * wide), BF16),
            pltpu.VMEM((size_x // 2, size_y // 2, size_z, wide), F32),
            pltpu.VMEM((size_x // 4, size_y // 4, size_z, wide), F32),
            pltpu.SemaphoreType.DMA((5, 8)),
            pltpu.SemaphoreType.DMA((5, 8)),
            pltpu.SemaphoreType.DMA((2, senders)),
            pltpu.SemaphoreType.DMA((2, senders)),
            pltpu.SemaphoreType.DMA((3,)),
        ],
        compiler_params=pltpu.CompilerParams(
            collective_id=0, has_side_effects=True, vmem_limit_bytes=56 * 1024 * 1024
        ),
        cost_estimate=pl.CostEstimate(
            flops=30_000_000_000, bytes_accessed=10_000_000, transcendentals=0
        ),
    )(
        records[0],
        slot_voxels[0],
        lift_weight,
        leaf_convs.reshape(2, 9, 3, channels, channels),
        down_leaf.reshape(4, 2 * channels, wide),
        down_coarse.reshape(2, 8, wide, wide),
        coarse_convs.reshape(3, 9, 3 * wide, wide),
        brick_mask,
    )
    return leaf, top


def solution(mesh):
    in_specs = (
        P(("gx", "gy"), None, None, None),
        P(("gx", "gy"), None, None),
        P("gx", "gy", None),
        P(),
        P(),
        P(),
        P(),
        P(),
    )
    out_specs = (P("gx", "gy", None, None), P("gx", "gy", None, None))
    return jax.shard_map(
        functools.partial(per_device, mesh.shape["gx"], mesh.shape["gy"]),
        mesh=mesh,
        in_specs=in_specs,
        out_specs=out_specs,
        check_vma=False,
    )
```

```python
import functools

import jax
import jax.numpy as jnp
from jax import lax
from jax.experimental import pallas as pl
from jax.experimental.pallas import tpu as pltpu
from jax.sharding import PartitionSpec as P

BRICK = 8
F32 = jnp.float32
BF16 = jnp.bfloat16
SIDES = [(-1, 0), (1, 0), (0, -1), (0, 1), (-1, -1), (-1, 1), (1, -1), (1, 1)]


def dot(left, right):
    return jnp.dot(left, right, preferred_element_type=F32)


def over(value, size):
    if size & (size - 1):
        return value // size
    return lax.shift_right_logical(value, jnp.full_like(value, size.bit_length() - 1))


def within(value, size):
    return value % size if size & (size - 1) else value & (size - 1)


def side_parts(count, here, other):
    near, far = 1, count
    own = {-1: near, 1: far, 0: pl.ds(1, count)}
    there = {-1: count + 1, 1: 0, 0: pl.ds(1, count)}
    return (own[here], own[other]), (there[here], there[other])


class Halo:
    def __init__(self, size_x, size_y, send_sems, recv_sems):
        self.place_x, self.place_y = lax.axis_index("gx"), lax.axis_index("gy")
        self.size_x, self.size_y = size_x, size_y
        self.send_sems, self.recv_sems = send_sems, recv_sems

    def each(self, action):
        for index, (step_x, step_y) in enumerate(SIDES):
            to_x, to_y = self.place_x + step_x, self.place_y + step_y
            tests = []
            if step_x:
                tests.append(to_x >= 0 if step_x < 0 else to_x < self.size_x)
            if step_y:
                tests.append(to_y >= 0 if step_y < 0 else to_y < self.size_y)
            exists = tests[0] if len(tests) == 1 else jnp.logical_and(*tests)

            @pl.when(exists)
            def _():
                action(index, step_x, step_y, (to_x, to_y))

    def copy(self, stage, buffer, index, step_x, step_y, target):
        source, landing = side_parts(buffer.shape[0] - 2, step_x, step_y)
        return pltpu.make_async_remote_copy(
            src_ref=buffer.at[source],
            dst_ref=buffer.at[landing],
            send_sem=self.send_sems.at[stage, index],
            recv_sem=self.recv_sems.at[stage, index],
            device_id=target,
            device_id_type=pl.DeviceIdType.MESH,
        )

    def start(self, stage, buffer):
        self.each(lambda *where: self.copy(stage, buffer, *where).start())

    def wait_arrived(self, stage, buffer):
        def arrived(index, step_x, step_y, target):
            opposite = SIDES.index((-step_x, -step_y))
            self.copy(stage, buffer, opposite, -step_x, -step_y, target).wait_recv()

        self.each(arrived)

    def wait_sent(self, stage, buffer):
        self.each(lambda *where: self.copy(stage, buffer, *where).wait_send())


def clear_border(buffer):
    last = buffer.shape[0] - 1
    edge = jnp.zeros(buffer.shape[1:], buffer.dtype)
    column = jnp.zeros((buffer.shape[0],) + buffer.shape[2:], buffer.dtype)
    buffer[0] = edge
    buffer[last] = edge
    buffer[:, 0] = column
    buffer[:, last] = column


def shift_rows(rows, period):
    count = rows.shape[0]
    z = within(lax.broadcasted_iota(jnp.int32, rows.shape, 0), period)
    before = jnp.where(z == 0, 0.0, pltpu.roll(rows, 1, 0))
    after = jnp.where(z == period - 1, 0.0, pltpu.roll(rows, count - 1, 0))
    return before, after


def store_leaf(buffer, at_x, at_y, rows, shape):
    before, after = shift_rows(rows, shape[2])
    lane = lax.broadcasted_iota(jnp.int32, rows.shape, 1)
    outer = jnp.where(lane < rows.shape[1] // 2, after, before)
    both = jnp.concatenate([rows, outer], -1).astype(BF16)
    buffer[at_x, at_y] = both.reshape(shape[:3] + (both.shape[-1],))


def stacked_z(values):
    shape = values.shape
    rows = values.reshape(-1, shape[-1])
    before, after = shift_rows(rows, shape[2])
    return jnp.concatenate([before, rows, after], -1).reshape(shape[:3] + (3 * shape[3],))


def pair_part(values, part_x, part_y):
    size_x, size_y = values.shape[:2]
    split = values.reshape((size_x // 2, 2, size_y // 2, 2) + values.shape[2:])
    return split[:, part_x, :, part_y]


def encoder(
    n_gx,
    n_gy,
    records,
    slots,
    lift_weight,
    leaf_convs,
    down_leaf,
    down_coarse_far,
    coarse_convs_far,
    brick_mask,
    leaf_out,
    top_out,
    occupied,
    arrived,
    slots_out,
    slots_in,
    taps,
    down_coarse,
    coarse_convs,
    summed,
    leaf_a,
    leaf_b,
    coarse_a,
    coarse_b,
    coarse_c,
    stacked,
    level_one,
    level_two,
    send_sems,
    recv_sems,
    owner_send_sems,
    owner_recv_sems,
    local_sems,
):
    halo = Halo(n_gx, n_gy, send_sems, recv_sems)
    senders = n_gx * n_gy
    me = halo.place_x * n_gy + halo.place_y
    weights = (
        pltpu.make_async_copy(down_coarse_far, down_coarse, local_sems.at[0]),
        pltpu.make_async_copy(coarse_convs_far, coarse_convs, local_sems.at[1]),
    )
    own_records = pltpu.make_async_copy(records.at[me], arrived.at[0], local_sems.at[2])
    own_records.start()

    def owner(away):
        index = lax.rem(me + away, senders)
        return index, (index // n_gy, lax.rem(index, n_gy))

    barrier = pltpu.get_barrier_semaphore()

    def greet(away, carry):
        pl.semaphore_signal(
            barrier, inc=1, device_id=owner(away)[1], device_id_type=pl.DeviceIdType.MESH
        )
        return carry

    for buffer in (leaf_a, leaf_b, coarse_a, coarse_b, coarse_c):
        clear_border(buffer)
    lax.fori_loop(1, senders, greet, 0)

    def stage_slots(step, carry):
        base = pl.multiple_of(step * 8, 8)
        index = slots[pl.ds(base, 8), :]
        for place in range(8):
            slots_out[base + place] = index[place : place + 1]
        return carry

    lax.fori_loop(0, senders // 8, stage_slots, 0)
    slots_in[0] = slots_out[me]
    pl.semaphore_wait(barrier, senders - 1)

    def owner_copies(away):
        index, target = owner(away)
        return (
            pltpu.make_async_remote_copy(
                src_ref=slots_out.at[index],
                dst_ref=slots_in.at[away],
                send_sem=owner_send_sems.at[0, away],
                recv_sem=owner_recv_sems.at[0, away],
                device_id=target,
                device_id_type=pl.DeviceIdType.MESH,
            ),
            pltpu.make_async_remote_copy(
                src_ref=records.at[index],
                dst_ref=arrived.at[away],
                send_sem=owner_send_sems.at[1, away],
                recv_sem=owner_recv_sems.at[1, away],
                device_id=target,
                device_id_type=pl.DeviceIdType.MESH,
            ),
        )

    def send_owner(away, carry):
        for copy in owner_copies(away):
            copy.start()
        return carry

    def owner_arrived(away, carry):
        for copy in owner_copies(away):
            copy.wait_recv()
        return carry

    def owner_sent(away, carry):
        for copy in owner_copies(away):
            copy.wait_send()
        return carry

    lax.fori_loop(1, senders, send_owner, 0)
    for copy in weights:
        copy.start()

    bricks_x, bricks_y, bricks_z = brick_mask.shape
    mask_rows, fine_rows = occupied.shape[2], leaf_out.shape[2]
    row = lax.broadcasted_iota(jnp.int32, (mask_rows, bricks_z), 0)
    brick = jnp.where(row < fine_rows, over(row, BRICK // 2), row - fine_rows)
    here = brick == lax.broadcasted_iota(jnp.int32, (mask_rows, bricks_z), 1)
    for brick_x in range(bricks_x):
        for brick_y in range(bricks_y):
            line = brick_mask[brick_x, brick_y : brick_y + 1, :].astype(F32)
            line = jnp.sum(jnp.where(here, line, 0.0), axis=1, keepdims=True)
            occupied[brick_x, brick_y] = jnp.broadcast_to(line, occupied.shape[2:])

    for layer in range(2):
        for step in range(9):
            low, mid, high = (leaf_convs[layer, step, tap] for tap in range(3))
            none = jnp.zeros_like(low)
            first = jnp.concatenate([mid, high, none, low], 0)
            second = jnp.concatenate([low, mid, high, none], 0)
            taps[layer, step] = jnp.concatenate([first, second], 1)

    slot_rows, width = arrived.shape[1:]
    cap = slots.shape[1]
    lanes = cap // slot_rows
    features = width // lanes
    span = summed.shape[1]
    rows_hi = summed.shape[0]
    group = 4
    order_from = lax.broadcasted_iota(jnp.int32, (cap, cap), 0)
    order_to = lax.broadcasted_iota(jnp.int32, (cap, cap), 1)
    order = jnp.where(
        order_from == within(order_to, slot_rows) * lanes + over(order_to, slot_rows), 1.0, 0.0
    ).astype(BF16)
    pick_from = lax.broadcasted_iota(jnp.int32, (width, lanes * span), 0)
    pick_to = lax.broadcasted_iota(jnp.int32, (width, lanes * span), 1)
    pick = jnp.where(
        pick_from == over(pick_to, span) * features + within(pick_to, features), 1.0, 0.0
    ).astype(BF16)
    column_group = over(lax.broadcasted_iota(jnp.int32, (cap, span), 1), features).astype(F32)
    row_index = lax.broadcasted_iota(jnp.int32, (rows_hi, cap), 0).astype(F32)
    summed[...] = jnp.zeros_like(summed)

    def add_group(step, carry):
        base = step * 8
        lax.fori_loop(jnp.where(step > 0, base, 1), base + 8, owner_arrived, 0)
        index = jnp.concatenate([slots_in[base + place] for place in range(8)], 0)
        wide_all = dot(arrived[pl.ds(base, 8)].reshape(8 * slot_rows, width), pick)
        high = within(over(index, 2), rows_hi)
        low = over(index, 2 * rows_hi) * 2 + within(index, 2)
        high_row = 64.0 * dot(over(high, 64).astype(F32).astype(BF16), order) + dot(
            within(high, 64).astype(F32).astype(BF16), order
        )
        low_column = lax.dot_general(
            order,
            low.astype(F32).astype(BF16),
            (((0,), (1,)), ((), ())),
            preferred_element_type=F32,
        )
        for part in range(8 // group):
            hots, tables = [], []
            for inner in range(group):
                place = part * group + inner
                hot = jnp.where(row_index == high_row[place : place + 1], 1.0, 0.0)
                hots.append(hot.astype(BF16))
                wide = wide_all[place * slot_rows : (place + 1) * slot_rows]
                wide = jnp.concatenate(
                    [wide[:, lane * span : (lane + 1) * span] for lane in range(lanes)], 0
                )
                tables.append(
                    jnp.where(column_group == low_column[:, place : place + 1], wide, 0.0).astype(
                        BF16
                    )
                )
            summed[...] += dot(jnp.concatenate(hots, 1), jnp.concatenate(tables, 0))
        return carry

    own_records.wait()
    lax.fori_loop(0, senders // 8, add_group, 0)

    size_x, size_y, size_z, leaf_width = leaf_out.shape
    quarter = rows_hi // (size_y * size_z)
    channels = lift_weight.shape[1]
    lift_shape = (span, span // features * channels)
    copy_rows = (
        within(lax.broadcasted_iota(jnp.int32, (span, features), 0), features)
        == lax.broadcasted_iota(jnp.int32, (span, features), 1)
    )
    copy_columns = (
        within(lax.broadcasted_iota(jnp.int32, (channels, lift_shape[1]), 1), channels)
        == lax.broadcasted_iota(jnp.int32, (channels, lift_shape[1]), 0)
    )
    lift = dot(jnp.where(copy_rows, 1.0, 0.0).astype(BF16), lift_weight[...])
    lift = dot(lift.astype(BF16), jnp.where(copy_columns, 1.0, 0.0).astype(BF16))
    on_block = (
        over(lax.broadcasted_iota(jnp.int32, lift_shape, 0), features)
        == over(lax.broadcasted_iota(jnp.int32, lift_shape, 1), channels)
    )
    lift = jnp.where(on_block, lift, 0.0).astype(BF16)
    rest = summed[...]
    lifted = 0.0
    for piece in range(3):
        cut = rest.astype(BF16)
        rest = rest - cut.astype(F32)
        lifted = lifted + dot(cut, lift)
    inside_y = pl.ds(1, size_y)
    for block in range(size_x // quarter):
        store_leaf(
            leaf_a,
            pl.ds(1 + block * quarter, quarter),
            inside_y,
            lifted[:, block * leaf_width : (block + 1) * leaf_width],
            (quarter, size_y, size_z),
        )

    halo.start(0, leaf_a)

    def convolve(source, layer, x, count_x, y, count_y):
        windows = []
        for step in range(9):
            window = source[pl.ds(x + step // 3, count_x), pl.ds(y + step % 3, count_y)]
            windows.append(window.reshape(-1, window.shape[-1]))
        table = taps[layer].reshape(-1, taps.shape[-1])
        return jnp.maximum(dot(jnp.concatenate(windows, -1), table), 0.0)

    def leaf_layer(source, layer, emit):
        def block(x, count_x, y, count_y):
            swept = convolve(source, layer, x, count_x, y, count_y)
            mask = jnp.concatenate(
                [
                    occupied[(x + step_x) // BRICK, (y + step_y) // BRICK, 0:size_z]
                    for step_x in range(count_x)
                    for step_y in range(count_y)
                ],
                0,
            )
            emit(x, count_x, y, count_y, swept * mask)

        def inner(step, carry):
            block(1 + 2 * step, 2, 1, size_y - 2)
            return carry

        lax.fori_loop(0, (size_x - 2) // 2, inner, 0)
        halo.wait_arrived(layer, source)
        block(0, 1, 0, size_y)
        block(size_x - 1, 1, 0, size_y)
        block(1, size_x - 2, 0, 1)
        block(1, size_x - 2, size_y - 1, 1)

    def keep_first(x, count_x, y, count_y, rows):
        store_leaf(
            leaf_b,
            pl.ds(1 + x, count_x),
            pl.ds(1 + y, count_y),
            rows,
            (count_x, count_y, size_z),
        )

    def keep_second(x, count_x, y, count_y, rows):
        leaf_out[pl.ds(x, count_x), pl.ds(y, count_y)] = rows.astype(BF16).reshape(
            count_x, count_y, size_z, leaf_width
        )

    leaf_layer(leaf_a, 0, keep_first)
    halo.start(1, leaf_b)
    leaf_layer(leaf_b, 1, keep_second)

    def widen(mask, factor):
        size = mask.shape[0] * factor
        return jnp.stack(
            [
                jnp.stack([mask[x // factor, y // factor] for y in range(size)])
                for x in range(size)
            ]
        )

    occ1 = widen(occupied[:, :, 0:size_z], BRICK // 2)
    occ2 = widen(occupied[:, :, pl.ds(0, size_z // 2, 2)], BRICK // 4)
    occ3 = occupied[:, :, size_z : size_z + size_z // 2]

    def coarse_conv(level, kernel, occupied):
        count, depth = kernel.shape[0] - 2, kernel.shape[2]
        total = None
        for step in range(9):
            step_x, step_y = step // 3, step % 3
            window = kernel[step_x : step_x + count, step_y : step_y + count]
            window = window.reshape(count * count * depth, window.shape[-1]).astype(BF16)
            term = dot(window, coarse_convs[level, step])
            total = term if total is None else total + term
        return jnp.maximum(total, 0.0).reshape(occupied.shape) * occupied

    def finish_down(stage, buffer, total, occupied):
        count = occupied.shape[0]
        cells = jnp.maximum(total, 0.0).reshape(occupied.shape) * occupied
        buffer[1 : count + 1, 1 : count + 1] = cells
        halo.start(stage, buffer)
        halo.wait_arrived(stage, buffer)

    for copy in weights:
        copy.wait()
    total = 0.0
    leaf = leaf_out[...]
    for part in range(4):
        piece = pair_part(leaf, part // 2, part % 2)
        total = total + dot(piece.reshape(-1, leaf_width), down_leaf[part])
    finish_down(2, coarse_a, total, occ1)
    stacked[...] = stacked_z(coarse_a[...]).astype(BF16)
    level_one[...] = coarse_conv(0, stacked, occ1)

    def shrink(level, source, depth):
        total = 0.0
        for part_z in range(2):
            half = source[:, :, pl.ds(part_z, depth, 2), :]
            for part in range(4):
                piece = pair_part(half, part // 2, part % 2)
                piece = piece.reshape(-1, piece.shape[-1]).astype(BF16)
                total = total + dot(piece, down_coarse[level, 2 * part + part_z])
        return total

    finish_down(3, coarse_b, shrink(0, level_one, occ2.shape[2]), occ2)
    deep = occ2.shape[2]
    level_two[:, :, deep : 2 * deep] = jnp.zeros_like(occ2)
    level_two[:, :, 0:deep] = coarse_conv(1, stacked_z(coarse_b[...]), occ2)
    finish_down(4, coarse_c, shrink(1, level_two, occ3.shape[2]), occ3)
    top = coarse_conv(2, stacked_z(coarse_c[...]), occ3)
    top_out[...] = top[:, :, 0 : top_out.shape[2]].astype(BF16)
    lax.fori_loop(1, senders, owner_sent, 0)

    for stage, buffer in enumerate((leaf_a, leaf_b, coarse_a, coarse_b, coarse_c)):
        halo.wait_sent(stage, buffer)


def per_device(
    n_gx,
    n_gy,
    records,
    slot_voxels,
    brick_mask,
    lift_weight,
    leaf_convs,
    down_leaf,
    down_coarse,
    coarse_convs,
):
    bricks_x, bricks_y, bricks_z = brick_mask.shape
    size_x, size_y, size_z = BRICK * bricks_x, BRICK * bricks_y, BRICK * bricks_z // 2
    features, channels = lift_weight.shape
    wide = down_leaf.shape[-1]
    rows_hi = size_x * size_y * size_z // 4
    span = 8 * features
    senders, slot_rows, width = records.shape[1:]
    cap = slot_voxels.shape[-1]
    far = pl.BlockSpec(memory_space=pl.ANY)
    vmem = pl.BlockSpec(memory_space=pltpu.VMEM)
    leaf, top = pl.pallas_call(
        functools.partial(encoder, n_gx, n_gy),
        out_shape=(
            jax.ShapeDtypeStruct((size_x, size_y, size_z, 2 * channels), BF16),
            jax.ShapeDtypeStruct((bricks_x, bricks_y, bricks_z, wide), BF16),
        ),
        in_specs=[far, vmem, vmem, vmem, vmem, far, far, vmem],
        out_specs=(vmem, vmem),
        scratch_shapes=[
            pltpu.VMEM((bricks_x, bricks_y, size_z + size_z // 2, 2 * channels), F32),
            pltpu.VMEM((senders, slot_rows, width), BF16),
            pltpu.VMEM((senders, 1, cap), jnp.int32),
            pltpu.VMEM((senders, 1, cap), jnp.int32),
            pltpu.VMEM((2, 9, 4 * channels, 2 * channels), BF16),
            pltpu.VMEM((2, 8, wide, wide), BF16),
            pltpu.VMEM((3, 9, 3 * wide, wide), BF16),
            pltpu.VMEM((rows_hi, span), F32),
            pltpu.VMEM((size_x + 2, size_y + 2, size_z, 4 * channels), BF16),
            pltpu.VMEM((size_x + 2, size_y + 2, size_z, 4 * channels), BF16),
            pltpu.VMEM((size_x // 2 + 2, size_y // 2 + 2, size_z, wide), F32),
            pltpu.VMEM((size_x // 4 + 2, size_y // 4 + 2, size_z // 2, wide), F32),
            pltpu.VMEM((size_x // 8 + 2, size_y // 8 + 2, size_z // 2, wide), F32),
            pltpu.VMEM((size_x // 2 + 2, size_y // 2 + 2, size_z, 3 * wide), BF16),
            pltpu.VMEM((size_x // 2, size_y // 2, size_z, wide), F32),
            pltpu.VMEM((size_x // 4, size_y // 4, size_z, wide), F32),
            pltpu.SemaphoreType.DMA((5, 8)),
            pltpu.SemaphoreType.DMA((5, 8)),
            pltpu.SemaphoreType.DMA((2, senders)),
            pltpu.SemaphoreType.DMA((2, senders)),
            pltpu.SemaphoreType.DMA((3,)),
        ],
        compiler_params=pltpu.CompilerParams(
            collective_id=0, has_side_effects=True, vmem_limit_bytes=56 * 1024 * 1024
        ),
        cost_estimate=pl.CostEstimate(
            flops=30_000_000_000, bytes_accessed=10_000_000, transcendentals=0
        ),
    )(
        records[0],
        slot_voxels[0],
        lift_weight,
        leaf_convs.reshape(2, 9, 3, channels, channels),
        down_leaf.reshape(4, 2 * channels, wide),
        down_coarse.reshape(2, 8, wide, wide),
        coarse_convs.reshape(3, 9, 3 * wide, wide),
        brick_mask,
    )
    return leaf, top


def solution(mesh):
    in_specs = (
        P(("gx", "gy"), None, None, None),
        P(("gx", "gy"), None, None),
        P("gx", "gy", None),
        P(),
        P(),
        P(),
        P(),
        P(),
    )
    out_specs = (P("gx", "gy", None, None), P("gx", "gy", None, None))
    return jax.shard_map(
        functools.partial(per_device, mesh.shape["gx"], mesh.shape["gy"]),
        mesh=mesh,
        in_specs=in_specs,
        out_specs=out_specs,
        check_vma=False,
    )
```
